32 devices in a mesh: sub: 8 (over z, core), front: 4 (over y, x).
Axes of the slice: x: 2, y: 2, z: 4, core: 2. Of those that a mesh axis runs over, the one named last changes fastest.
Arguments:
- noise_root: float32 [16, 128, 256], P('front', 'sub'), may hold values from -6 to 6
- inverse_root: float32 [16, 256, 256], P('front'), may hold values from -0.125 to 1.6, as said below
- up_root: float32 [16, 256, 128], P('front'), may hold values from -0.1875 to 0.1875
- left_root: float32 [16, 256, 128], P('front'), may hold values from -0.5 to 0.5
- rank_root: int32 [4], P('front'), may hold values from 64 to 128
- basis_root: float32 [16, 256, 128], P('front'), may hold values from -0.1875 to 0.1875
- noise_child: float32 [256, 128, 256], P(('sub', 'front')), may hold values from -6 to 6
- inverse_child: float32 [256, 256, 256], P(('sub', 'front')), may hold values from -0.125 to 1.6, as said below
- up_child: float32 [256, 256, 128], P(('sub', 'front')), may hold values from -0.125 to 0.125
- left_child: float32 [256, 256, 128], P(('sub', 'front')), may hold values from -0.5 to 0.5
- rank_child: int32 [32], P(('sub', 'front')), may hold values from 64 to 128
- couple: float32 [32, 4, 8, 256, 128], P(('sub', 'front')), may hold values from -0.125 to 0.125
- pattern: int32 [32, 4], P(('sub', 'front')), may hold values from 0 to 3, as said below
- couple_rank: int32 [32, 4], P(('sub', 'front')), may hold values from 64 to 128
Outputs:
- solved_root: float32 [16, 128, 256], P('front', 'sub')
- solved_child: float32 [256, 128, 256], P(('sub', 'front'))
The draws below stay inside these ranges and needn't reach their ends.
Inputs may be any that keep to these rules, and one draw needn't show every extreme that they name: `pattern`: each row names 4 different root panels, the first being the row's own panel index (row modulo 4). `inverse_root`: each tile is lower triangular with a positive diagonal. `inverse_child`: each tile is lower triangular with a positive diagonal.
All inputs are finite; a program needn't handle non-finite values.
Results may differ from the reference program's by a relative error of at most 0.00022.
Values sent between devices are 32-bit elements; how exact they have to be, the bound alone decides.
A program may use at most 64 MiB of HBM per device.

```python
import math
import jax
import jax.numpy as jnp
from jax import lax

B = 256
K = 128
NNZ = 4
T0 = 4
T1 = 8
NS = 128
N0 = 16
PANELS = 32
N1T = 256
N_SUB = 8
N_FRONT = 4


def lower_tiles(key, tile_count, bottom, ceiling):
    first_key, second_key = jax.random.split(key)
    row_index = lax.broadcasted_iota(jnp.int32, (tile_count, B, B), 1)
    column_index = lax.broadcasted_iota(jnp.int32, (tile_count, B, B), 2)
    diagonal = jax.random.uniform(first_key, (tile_count, B, B), jnp.float32, bottom, ceiling)
    below_part = jnp.clip(jax.random.normal(second_key, (tile_count, B, B), jnp.float32) * (0.5 / math.sqrt(B)), -0.125, 0.125)
    return jnp.where(row_index == column_index, diagonal, jnp.where(row_index > column_index, below_part, 0.0))


def draw_inverse_root(key, part):
    key = jax.random.fold_in(key, 11)
    return lower_tiles(key, N0, 0.7, 1.4)


def draw_inverse_child(key, part):
    key = jax.random.fold_in(key, 23)
    return lower_tiles(key, N1T, 0.7, 1.4)


def draw_pattern(key, part):
    key = jax.random.fold_in(key, 37)
    column_index = lax.broadcasted_iota(jnp.int32, (PANELS, N_FRONT), 1)
    own_panel = lax.broadcasted_iota(jnp.int32, (PANELS, N_FRONT), 0) % N_FRONT
    scores = jax.random.randint(key, (PANELS, N_FRONT), 0, 1 << 20) * N_FRONT + column_index
    scores = jnp.where(column_index == own_panel, -1, scores)
    ordered = jnp.argsort(scores, axis=1, stable=True)
    return ordered[:, :NNZ].astype(jnp.int32)


def with_ends(entries, rng, smallest, high):
    index_at = [jax.random.randint(jax.random.fold_in(rng, axis), (), 0, length) for axis, length in enumerate(entries.shape)]
    longest = entries.shape.index(max(entries.shape))
    next_to = index_at[:longest] + [(index_at[longest] + 1) % entries.shape[longest]] + index_at[longest + 1:]
    return entries.at[tuple(index_at)].set(smallest).at[tuple(next_to)].set(high)


def level_of(key, dims, cuts, smallest, top_value):
    gain, own = 1.0, jax.random.fold_in(key, 6)
    for position, shards_of in cuts:
        draws = jnp.exp(jax.random.uniform(jax.random.fold_in(own, position), (shards_of,), jnp.float32, smallest / len(cuts), top_value / len(cuts)))
        gain = gain * jnp.repeat(draws, dims[position] // shards_of).reshape([-1 if axis == position else 1 for axis in range(len(dims))])
    return gain


def centred(rng, shape, spread, limit, cuts=(), kind=jnp.bfloat16):
    values = jax.random.normal(rng, shape, jnp.float32) * spread
    if len(cuts) > 0:
        values = level_of(rng, shape, cuts, -0.22, 0.18) * values
    return jnp.clip(values, min=-limit, max=limit).astype(kind)


def setup_inputs(seed: int = 0) -> dict:
    key_of = jax.random.split(jax.random.key(seed), 15)
    return {
        "noise_root": centred(key_of[0], (N0, NS, B), 1.0, 6.0, ((0, 4), (1, 8)), jnp.float32),
        "inverse_root": draw_inverse_root(jax.random.fold_in(key_of[14], 71), 0),
        "up_root": centred(key_of[2], (N0, B, K), (T0 * B) ** -0.5, 0.1875, ((0, 4),), jnp.float32),
        "left_root": centred(key_of[3], (N0, B, K), K ** -0.5, 0.5, ((0, 4),), jnp.float32),
        "rank_root": with_ends(jax.random.randint(key_of[4], (N_FRONT,), K // 2, K + 1), jax.random.fold_in(key_of[4], 1), K // 2, K).astype(jnp.int32),
        "basis_root": centred(key_of[5], (N0, B, K), (T0 * B) ** -0.5, 0.1875, ((0, 4),), jnp.float32),
        "noise_child": centred(key_of[6], (N1T, NS, B), 1.0, 6.0, ((0, 32),), jnp.float32),
        "inverse_child": draw_inverse_child(jax.random.fold_in(key_of[14], 71), 0),
        "up_child": centred(key_of[8], (N1T, B, K), (T1 * B) ** -0.5, 0.125, ((0, 32),), jnp.float32),
        "left_child": centred(key_of[9], (N1T, B, K), K ** -0.5, 0.5, ((0, 32),), jnp.float32),
        "rank_child": with_ends(jax.random.randint(key_of[10], (PANELS,), K // 2, K + 1), jax.random.fold_in(key_of[10], 1), K // 2, K).astype(jnp.int32),
        "couple": centred(key_of[11], (PANELS, NNZ, T1, B, K), (4 * NNZ * K) ** -0.5, 0.125, ((0, 32),), jnp.float32),
        "pattern": draw_pattern(jax.random.fold_in(key_of[14], 71), 0),
        "couple_rank": with_ends(jax.random.randint(key_of[13], (PANELS, NNZ), K // 2, K + 1), jax.random.fold_in(key_of[13], 1), K // 2, K).astype(jnp.int32),
    }


PRECISE = lax.Precision.HIGHEST


def keep_mask(rank_cut, width):
    levels = lax.broadcasted_iota(jnp.int32, rank_cut.shape + (width,), rank_cut.ndim)
    return (levels < rank_cut[..., None]).astype(jnp.float32)


def chain_solve(source, inverse, upward, leftward, keeper, tile_count):
    panels = source.shape[0] // tile_count

    def shaped(array):
        return array.reshape((panels, tile_count) + array.shape[1:])

    def advance(message, pieces):
        source_part, inverse_part, upward_part, leftward_part, keeper_part = pieces
        carried = jnp.einsum("sk,tbk->tsb", message, leftward_part, precision=PRECISE)
        solved = jnp.einsum("tsb,tbc->tsc", source_part - carried, inverse_part, precision=PRECISE)
        message = jnp.einsum("tsc,tck->sk", solved, upward_part, precision=PRECISE) * keeper_part
        return message, solved

    start_message = jnp.zeros((source.shape[1], upward.shape[-1]), jnp.float32)
    final_message, solved = lax.scan(advance, start_message, (shaped(source), shaped(inverse), shaped(upward), shaped(leftward), keeper), reverse=True)
    return solved.reshape(source.shape)


def reference(noise_root, inverse_root, up_root, left_root, rank_root, basis_root, noise_child, inverse_child, up_child, left_child, rank_child, couple, pattern, couple_rank):
    solved_root = chain_solve(noise_root, inverse_root, up_root, left_root, keep_mask(rank_root, K), T0)
    projected = jnp.einsum("ptsb,ptbk->psk", solved_root.reshape(N_FRONT, T0, NS, B), basis_root.reshape(N_FRONT, T0, B, K), precision=PRECISE)
    chosen = projected[pattern] * keep_mask(couple_rank, K)[:, :, None, :]
    update = jnp.einsum("rmsk,rmtbk->rtsb", chosen, couple, precision=PRECISE)
    source = noise_child - update.reshape(noise_child.shape)
    child_keep = keep_mask(rank_child, K).reshape(N_SUB, N_FRONT, K)

    def one_separator(pieces):
        return chain_solve(pieces[0], pieces[1], pieces[2], pieces[3], pieces[4], T1)

    solved_child = lax.map(one_separator, (source.reshape(N_SUB, N_FRONT * T1, NS, B), inverse_child.reshape(N_SUB, N_FRONT * T1, B, B), up_child.reshape(N_SUB, N_FRONT * T1, B, K), left_child.reshape(N_SUB, N_FRONT * T1, B, K), child_keep))
    return solved_root, solved_child.reshape(noise_child.shape)
```

```python
import functools

import jax
import jax.numpy as jnp
from jax import lax
from jax.experimental import pallas as pl
from jax.experimental.pallas import tpu as pltpu
from jax.sharding import PartitionSpec as P

F32 = jnp.float32
BF16 = jnp.bfloat16
NN = ((1,), (0,))
NT = ((1,), (1,))


def split(value):
    high = value.astype(BF16)
    return high, (value - high.astype(F32)).astype(BF16)


def dot3(left, right, contract):
    def one(x, y):
        return lax.dot_general(x, y, (contract, ((), ())), preferred_element_type=F32)

    return one(left[0], right[0]) + (one(left[0], right[1]) + one(left[1], right[0]))


def dot(left, right, contract):
    return dot3(split(left), split(right), contract)


def kernel(
    front_count,
    sub_count,
    rank_root,
    rank_child,
    pattern,
    couple_rank,
    noise_root_hbm,
    inverse_root_hbm,
    up_root_hbm,
    left_root_hbm,
    basis_root_hbm,
    noise_child_hbm,
    inverse_child_hbm,
    up_child_hbm,
    left_child_hbm,
    couple_hbm,
    solved_root_hbm,
    solved_child_hbm,
    noise_root,
    inverse_root,
    up_root,
    left_root,
    basis_root,
    noise_child,
    inverse_child,
    up_child,
    left_child,
    couple,
    solved_root,
    solved_child,
    root_mixing,
    root_message,
    root_outgoing,
    projected,
    child_opening,
    child_factor,
    carried,
    mixings,
    openings,
    message,
    load_sem,
    store_sem,
    chain_sem,
    sub_send,
    sub_recv,
    front_send,
    front_recv,
    mixing_send,
    mixing_recv,
    opening_send,
    opening_recv,
):
    sub = lax.axis_index("sub")
    front = lax.axis_index("front")
    root_tiles, share, _ = noise_root.shape
    child_tiles = noise_child.shape[0]
    width = up_root.shape[-1]
    couplings = couple.shape[0]
    last = front_count - 1

    loads = {}
    for index, (name, source, target) in enumerate((
        ("inverse_root", inverse_root_hbm, inverse_root),
        ("up_root", up_root_hbm, up_root),
        ("basis_root", basis_root_hbm, basis_root),
        ("noise_root", noise_root_hbm, noise_root),
        ("left_root", left_root_hbm, left_root),
        ("inverse_child", inverse_child_hbm, inverse_child),
        ("up_child", up_child_hbm, up_child),
        ("noise_child", noise_child_hbm, noise_child),
        ("left_child", left_child_hbm, left_child),
        ("couple", couple_hbm.at[0], couple),
    )):
        loads[name] = pltpu.make_async_copy(source, target, load_sem.at[index])
        loads[name].start()

    barrier = pltpu.get_barrier_semaphore()
    for step in range(1, sub_count):
        pl.semaphore_signal(
            barrier, inc=1, device_id={"sub": lax.rem(sub + step, sub_count)}, device_id_type=pl.DeviceIdType.MESH
        )
    for step in range(1, front_count):
        pl.semaphore_signal(
            barrier, inc=1, device_id={"front": lax.rem(front + step, front_count)}, device_id_type=pl.DeviceIdType.MESH
        )

    lanes = lax.broadcasted_iota(jnp.int32, (1, width), 1)
    rows = lax.broadcasted_iota(jnp.int32, (width, width), 0)
    root_keep = (lanes < rank_root[0]).astype(F32)
    child_keep = (lanes < rank_child[0]).astype(F32)

    def remote(source, target, send, recv, axis, peer):
        return pltpu.make_async_remote_copy(
            src_ref=source,
            dst_ref=target,
            send_sem=send,
            recv_sem=recv,
            device_id={axis: peer},
            device_id_type=pl.DeviceIdType.MESH,
        )

    for name in ("inverse_root", "up_root", "basis_root", "noise_root"):
        loads[name].wait()
    solved_bases = []
    opening = jnp.zeros((share, 2 * width), F32)
    for tile in range(root_tiles):
        bases = jnp.concatenate([up_root[tile], basis_root[tile]], axis=1)
        solved_basis = dot(inverse_root[tile], bases, NN)
        opening = opening + dot(noise_root[tile], solved_basis, NN)
        solved_bases.append(solved_basis)
    pl.semaphore_wait(barrier, sub_count + front_count - 2)

    chain = remote(
        root_outgoing, root_message, chain_sem.at[0], chain_sem.at[1], "front", lax.rem(front + last, front_count)
    )

    @pl.when(front == last)
    def _():
        root_message[...] = jnp.zeros_like(root_message)
        root_outgoing[...] = root_keep * opening[:, :width]
        chain.start()

    loads["left_root"].wait()
    mixing = jnp.zeros((2 * width, width), F32)
    for tile in range(root_tiles):
        mixing = mixing + dot(solved_bases[tile].T, left_root[tile], NN)
    root_mixing[...] = mixing

    @pl.when(front < last)
    def _():
        chain.wait_recv()

    arrived = root_message[...]
    both = opening - dot(arrived, root_mixing[...], NT)

    @pl.when(jnp.logical_and(front < last, front > 0))
    def _():
        root_outgoing[...] = root_keep * both[:, :width]
        chain.start()

    mine = pl.ds(pl.multiple_of(sub * share, share), share)
    projected[front, mine, :] = both[:, width:]
    for step in range(1, sub_count):
        block = projected.at[front, mine, :]
        remote(block, block, sub_send.at[step], sub_recv.at[sub], "sub", lax.rem(sub + step, sub_count)).start()

    for name in ("inverse_child", "up_child", "noise_child", "left_child", "couple"):
        loads[name].wait()
    child_opening[...] = jnp.zeros_like(child_opening)
    child_factor[...] = jnp.zeros_like(child_factor)

    def prepare(tile, _):
        solved_basis = dot(inverse_child[tile], up_child[tile], NN)
        child_opening[...] += dot(noise_child[tile], solved_basis, NN)
        columns = jnp.concatenate([left_child[tile]] + [couple[m, tile] for m in range(couplings)], axis=1)
        child_factor[...] += dot(solved_basis.T, columns, NN)
        return 0

    lax.fori_loop(0, child_tiles // 2, prepare, 0)

    for step in range(1, sub_count):
        peer = lax.rem(sub + step, sub_count)
        block = projected.at[front, pl.ds(pl.multiple_of(peer * share, share), share), :]
        remote(block, block, sub_send.at[step], sub_recv.at[peer], "sub", peer).wait_recv()
    for step in range(1, front_count):
        block = projected.at[front]
        remote(
            block, block, front_send.at[step], front_recv.at[front], "front", lax.rem(front + step, front_count)
        ).start()

    lax.fori_loop(child_tiles // 2, child_tiles, prepare, 0)

    mixings[front] = jnp.where(rows < rank_child[0], -child_factor[:, :width], 0.0)
    for peer in range(last):

        @pl.when(jnp.logical_and(peer < front, front < last))
        def _():
            block = mixings.at[front]
            remote(block, block, mixing_send.at[peer], mixing_recv.at[front], "front", peer).start()

    for tile in range(root_tiles):
        reduced = noise_root[tile] - dot(arrived, left_root[tile], NT)
        solved_root[tile] = dot(reduced, inverse_root[tile], NN)
    root_store = pltpu.make_async_copy(solved_root, solved_root_hbm, store_sem.at[0])
    root_store.start()

    for step in range(1, front_count):
        peer = lax.rem(front + step, front_count)
        block = projected.at[peer]
        remote(block, block, front_send.at[step], front_recv.at[peer], "front", peer).wait_recv()

    chosen = jnp.concatenate(
        [
            projected[pattern[0, m]] * (lanes < couple_rank[0, m]).astype(F32)
            for m in range(couplings)
        ],
        axis=1,
    )
    chosen = split(chosen)
    openings[front] = child_keep * (child_opening[...] - dot3(chosen, split(child_factor[:, width:]), NT))
    for peer in range(last):

        @pl.when(peer < front)
        def _():
            block = openings.at[front]
            remote(block, block, opening_send.at[peer], opening_recv.at[front], "front", peer).start()

    def solve(tile, _):
        inverse = split(inverse_child[tile])
        columns = jnp.concatenate([couple[m, tile] for m in range(couplings)], axis=1)
        source = noise_child[tile] - dot3(chosen, split(columns), NT)
        solved_child[tile] = dot3(split(source), inverse, NN)
        carried[tile] = dot3(split(left_child[tile].T), inverse, NN)
        return 0

    lax.fori_loop(0, child_tiles, solve, 0)

    message[...] = jnp.zeros_like(message)
    for panel in range(last, 0, -1):

        @pl.when(front < panel)
        def _():
            if panel < last:
                block = mixings.at[panel]
                remote(block, block, mixing_send.at[0], mixing_recv.at[panel], "front", panel).wait_recv()
            block = openings.at[panel]
            remote(block, block, opening_send.at[0], opening_recv.at[panel], "front", panel).wait_recv()
            if panel < last:
                message[...] = openings[panel] + dot(message[...], mixings[panel], NT)
            else:
                message[...] = openings[panel]

    incoming = split(message[...])
    stores = []
    for tile in range(child_tiles):
        solved_child[tile] -= dot3(incoming, split(carried[tile]), NN)
        stores.append(pltpu.make_async_copy(solved_child.at[tile], solved_child_hbm.at[tile], store_sem.at[1 + tile]))
        stores[-1].start()

    @pl.when(front > 0)
    def _():
        chain.wait_send()

    for step in range(1, sub_count):
        block = projected.at[front, mine, :]
        remote(block, block, sub_send.at[step], sub_recv.at[sub], "sub", lax.rem(sub + step, sub_count)).wait_send()
    for step in range(1, front_count):
        block = projected.at[front]
        remote(
            block, block, front_send.at[step], front_recv.at[front], "front", lax.rem(front + step, front_count)
        ).wait_send()
    for peer in range(last):

        @pl.when(jnp.logical_and(peer < front, front < last))
        def _():
            block = mixings.at[front]
            remote(block, block, mixing_send.at[peer], mixing_recv.at[front], "front", peer).wait_send()

        @pl.when(peer < front)
        def _():
            block = openings.at[front]
            remote(block, block, opening_send.at[peer], opening_recv.at[front], "front", peer).wait_send()

    root_store.wait()
    for store in stores:
        store.wait()


def body(
    front_count,
    sub_count,
    noise_root,
    inverse_root,
    up_root,
    left_root,
    rank_root,
    basis_root,
    noise_child,
    inverse_child,
    up_child,
    left_child,
    rank_child,
    couple,
    pattern,
    couple_rank,
):
    share = noise_root.shape[1]
    child_tiles, samples, _ = noise_child.shape
    order, width = up_root.shape[1:]
    couplings = couple.shape[1]
    arrays = (
        noise_root,
        inverse_root,
        up_root,
        left_root,
        basis_root,
        noise_child,
        inverse_child,
        up_child,
        left_child,
        couple,
    )
    dma = pltpu.SemaphoreType.DMA
    return pl.pallas_call(
        functools.partial(kernel, front_count, sub_count),
        out_shape=(
            jax.ShapeDtypeStruct(noise_root.shape, F32),
            jax.ShapeDtypeStruct(noise_child.shape, F32),
        ),
        in_specs=[pl.BlockSpec(memory_space=pltpu.SMEM)] * 4 + [pl.BlockSpec(memory_space=pl.ANY)] * len(arrays),
        out_specs=(pl.BlockSpec(memory_space=pl.ANY), pl.BlockSpec(memory_space=pl.ANY)),
        scratch_shapes=[pltpu.VMEM(array.shape, F32) for array in arrays[:-1]]
        + [
            pltpu.VMEM(couple.shape[1:], F32),
            pltpu.VMEM(noise_root.shape, F32),
            pltpu.VMEM(noise_child.shape, F32),
            pltpu.VMEM((2 * width, width), F32),
            pltpu.VMEM((share, width), F32),
            pltpu.VMEM((share, width), F32),
            pltpu.VMEM((front_count, samples, width), F32),
            pltpu.VMEM((samples, width), F32),
            pltpu.VMEM((width, (1 + couplings) * width), F32),
            pltpu.VMEM((child_tiles, width, order), F32),
            pltpu.VMEM((front_count, width, width), F32),
            pltpu.VMEM((front_count, samples, width), F32),
            pltpu.VMEM((samples, width), F32),
            dma((len(arrays),)),
            dma((1 + child_tiles,)),
            dma((2,)),
            dma((sub_count,)),
            dma((sub_count,)),
            dma((front_count,)),
            dma((front_count,)),
            dma((front_count,)),
            dma((front_count,)),
            dma((front_count,)),
            dma((front_count,)),
        ],
        compiler_params=pltpu.CompilerParams(
            collective_id=0, has_side_effects=True, vmem_limit_bytes=52 * 1024 * 1024
        ),
        name="matern_sample",
    )(rank_root, rank_child, pattern, couple_rank, *arrays)


def solution(mesh):
    placed = (
        P("front", "sub", None),
        P("front", None, None),
        P("front", None, None),
        P("front", None, None),
        P("front"),
        P("front", None, None),
        P(("sub", "front"), None, None),
        P(("sub", "front"), None, None),
        P(("sub", "front"), None, None),
        P(("sub", "front"), None, None),
        P(("sub", "front")),
        P(("sub", "front"), None, None, None, None),
        P(("sub", "front"), None),
        P(("sub", "front"), None),
    )
    return jax.shard_map(
        functools.partial(body, mesh.shape["front"], mesh.shape["sub"]),
        mesh=mesh,
        in_specs=placed,
        out_specs=(P("front", "sub", None), P(("sub", "front"), None, None)),
        check_vma=False,
    )
```

```python
import functools

import jax
import jax.numpy as jnp
from jax import lax
from jax.experimental import pallas as pl
from jax.experimental.pallas import tpu as pltpu
from jax.sharding import PartitionSpec as P

F32 = jnp.float32
BF16 = jnp.bfloat16
NN = ((1,), (0,))
NT = ((1,), (1,))


def split(value):
    high = value.astype(BF16)
    return high, (value - high.astype(F32)).astype(BF16)


def dot3(left, right, contract):
    def one(x, y):
        return lax.dot_general(x, y, (contract, ((), ())), preferred_element_type=F32)

    rows = left[0].shape[0]
    side = 1 - contract[1][0]
    columns = right[0].shape[side]
    stacked = jnp.concatenate(left, axis=0)
    if columns <= 128:
        both = one(stacked, jnp.concatenate(right, axis=side))
        return both[:rows, :columns] + (both[rows:, :columns] + both[:rows, columns:])
    both = one(stacked, right[0])
    return both[:rows] + (both[rows:] + one(left[0], right[1]))


def dot(left, right, contract):
    return dot3(split(left), split(right), contract)


def kernel(
    front_count,
    sub_count,
    rank_root_hbm,
    rank_child_hbm,
    pattern_hbm,
    couple_rank_hbm,
    noise_root_hbm,
    inverse_root_hbm,
    up_root_hbm,
    left_root_hbm,
    basis_root_hbm,
    noise_child_hbm,
    inverse_child_hbm,
    up_child_hbm,
    left_child_hbm,
    couple_hbm,
    solved_root_hbm,
    solved_child_hbm,
    rank_root,
    rank_child,
    pattern,
    couple_rank,
    noise_root,
    inverse_root,
    up_root,
    left_root,
    basis_root,
    noise_child,
    inverse_child,
    up_child,
    left_child,
    couple,
    solved_root,
    solved_child,
    root_mixing,
    root_message,
    root_outgoing,
    projected,
    child_opening,
    child_factor,
    carried_high,
    carried_low,
    mixings,
    openings,
    message,
    load_sem,
    store_sem,
    chain_sem,
    sub_send,
    sub_recv,
    front_send,
    front_recv,
    mixing_send,
    mixing_recv,
    opening_send,
    opening_recv,
):
    sub = lax.axis_index("sub")
    front = lax.axis_index("front")
    root_tiles, share, _ = noise_root.shape
    child_tiles = noise_child.shape[0]
    width = up_root.shape[-1]
    couplings = couple.shape[0]
    last = front_count - 1

    loads = {}
    for index, (name, source, target) in enumerate((
        ("rank_root", rank_root_hbm, rank_root),
        ("rank_child", rank_child_hbm, rank_child),
        ("pattern", pattern_hbm, pattern),
        ("couple_rank", couple_rank_hbm, couple_rank),
        ("inverse_root", inverse_root_hbm, inverse_root),
        ("up_root", up_root_hbm, up_root),
        ("basis_root", basis_root_hbm, basis_root),
        ("noise_root", noise_root_hbm, noise_root),
        ("left_root", left_root_hbm, left_root),
        ("inverse_child", inverse_child_hbm, inverse_child),
        ("up_child", up_child_hbm, up_child),
        ("noise_child", noise_child_hbm, noise_child),
        ("left_child", left_child_hbm, left_child),
        ("couple", couple_hbm.at[0], couple),
    )):
        loads[name] = pltpu.make_async_copy(source, target, load_sem.at[index])
        loads[name].start()

    barrier = pltpu.get_barrier_semaphore()
    for step in range(1, sub_count):
        pl.semaphore_signal(
            barrier, inc=1, device_id={"sub": lax.rem(sub + step, sub_count)}, device_id_type=pl.DeviceIdType.MESH
        )
    for step in range(1, front_count):
        pl.semaphore_signal(
            barrier, inc=1, device_id={"front": lax.rem(front + step, front_count)}, device_id_type=pl.DeviceIdType.MESH
        )

    lanes = lax.broadcasted_iota(jnp.int32, (1, width), 1)
    rows = lax.broadcasted_iota(jnp.int32, (width, width), 0)
    for name in ("rank_root", "rank_child", "pattern", "couple_rank"):
        loads[name].wait()
    root_keep = (lanes < rank_root[0]).astype(F32)
    child_keep = (lanes < rank_child[0]).astype(F32)

    def remote(source, target, send, recv, axis, peer):
        return pltpu.make_async_remote_copy(
            src_ref=source,
            dst_ref=target,
            send_sem=send,
            recv_sem=recv,
            device_id={axis: peer},
            device_id_type=pl.DeviceIdType.MESH,
        )

    for name in ("inverse_root", "up_root", "basis_root", "noise_root"):
        loads[name].wait()
    solved_bases = []
    opening = jnp.zeros((share, 2 * width), F32)
    for tile in range(root_tiles):
        bases = jnp.concatenate([up_root[tile], basis_root[tile]], axis=1)
        solved_basis = dot(inverse_root[tile], bases, NN)
        opening = opening + dot(noise_root[tile], solved_basis, NN)
        solved_bases.append(solved_basis)
    pl.semaphore_wait(barrier, sub_count + front_count - 2)

    chain = remote(
        root_outgoing, root_message, chain_sem.at[0], chain_sem.at[1], "front", lax.rem(front + last, front_count)
    )

    @pl.when(front == last)
    def _():
        root_message[...] = jnp.zeros_like(root_message)
        root_outgoing[...] = root_keep * opening[:, :width]
        chain.start()

    loads["left_root"].wait()
    mixing = jnp.zeros((2 * width, width), F32)
    for tile in range(root_tiles):
        mixing = mixing + dot(solved_bases[tile].T, left_root[tile], NN)
    root_mixing[...] = mixing

    @pl.when(front < last)
    def _():
        chain.wait_recv()

    arrived = root_message[...]
    both = opening - dot(arrived, root_mixing[...], NT)

    @pl.when(jnp.logical_and(front < last, front > 0))
    def _():
        root_outgoing[...] = root_keep * both[:, :width]
        chain.start()

    mine = pl.ds(pl.multiple_of(sub * share, share), share)
    projected[front, mine, :] = both[:, width:]
    for step in range(1, sub_count):
        block = projected.at[front, mine, :]
        remote(block, block, sub_send.at[step], sub_recv.at[sub], "sub", lax.rem(sub + step, sub_count)).start()

    for name in ("inverse_child", "up_child", "noise_child", "left_child", "couple"):
        loads[name].wait()
    child_opening[...] = jnp.zeros_like(child_opening)
    child_factor[...] = jnp.zeros_like(child_factor)

    def prepare(tile, _):
        solved_basis = dot(inverse_child[tile], up_child[tile], NN)
        child_opening[...] += dot(noise_child[tile], solved_basis, NN)
        columns = jnp.concatenate([left_child[tile]] + [couple[m, tile] for m in range(couplings)], axis=1)
        child_factor[...] += dot(solved_basis.T, columns, NN)
        return 0

    lax.fori_loop(0, child_tiles // 2, prepare, 0)

    for step in range(1, sub_count):
        peer = lax.rem(sub + step, sub_count)
        block = projected.at[front, pl.ds(pl.multiple_of(peer * share, share), share), :]
        remote(block, block, sub_send.at[step], sub_recv.at[peer], "sub", peer).wait_recv()
    for step in range(1, front_count):
        block = projected.at[front]
        remote(
            block, block, front_send.at[step], front_recv.at[front], "front", lax.rem(front + step, front_count)
        ).start()

    lax.fori_loop(child_tiles // 2, child_tiles, prepare, 0)

    mixings[front] = jnp.where(rows < rank_child[0], -child_factor[:, :width], 0.0)
    for peer in range(last):

        @pl.when(jnp.logical_and(peer < front, front < last))
        def _():
            block = mixings.at[front]
            remote(block, block, mixing_send.at[peer], mixing_recv.at[front], "front", peer).start()

    for tile in range(root_tiles):
        reduced = noise_root[tile] - dot(arrived, left_root[tile], NT)
        solved_root[tile] = dot(reduced, inverse_root[tile], NN)
    root_store = pltpu.make_async_copy(solved_root, solved_root_hbm, store_sem.at[0])
    root_store.start()

    for step in range(1, front_count):
        peer = lax.rem(front + step, front_count)
        block = projected.at[peer]
        remote(block, block, front_send.at[step], front_recv.at[peer], "front", peer).wait_recv()

    chosen = jnp.concatenate(
        [
            projected[pattern[0, m]] * (lanes < couple_rank[0, m]).astype(F32)
            for m in range(couplings)
        ],
        axis=1,
    )
    chosen = split(chosen)
    openings[front] = child_keep * (child_opening[...] - dot3(chosen, split(child_factor[:, width:]), NT))
    for peer in range(last):

        @pl.when(peer < front)
        def _():
            block = openings.at[front]
            remote(block, block, opening_send.at[peer], opening_recv.at[front], "front", peer).start()

    def solve(tile, _):
        inverse = split(inverse_child[tile])
        columns = jnp.concatenate([couple[m, tile] for m in range(couplings)], axis=1)
        source = noise_child[tile] - dot3(chosen, split(columns), NT)
        together = dot3(split(jnp.concatenate([source, left_child[tile].T], axis=0)), inverse, NN)
        solved_child[tile] = together[: source.shape[0]]
        carried_high[tile], carried_low[tile] = split(together[source.shape[0] :])
        return 0

    lax.fori_loop(0, child_tiles, solve, 0)

    message[...] = jnp.zeros_like(message)
    for panel in range(last, 0, -1):

        @pl.when(front < panel)
        def _():
            if panel < last:
                block = mixings.at[panel]
                remote(block, block, mixing_send.at[0], mixing_recv.at[panel], "front", panel).wait_recv()
            block = openings.at[panel]
            remote(block, block, opening_send.at[0], opening_recv.at[panel], "front", panel).wait_recv()
            if panel < last:
                message[...] = openings[panel] + dot(message[...], mixings[panel], NT)
            else:
                message[...] = openings[panel]

    incoming = split(message[...])
    stores = []
    for tile in range(child_tiles):
        solved_child[tile] -= dot3(incoming, (carried_high[tile], carried_low[tile]), NN)
        stores.append(pltpu.make_async_copy(solved_child.at[tile], solved_child_hbm.at[tile], store_sem.at[1 + tile]))
        stores[-1].start()

    @pl.when(front > 0)
    def _():
        chain.wait_send()

    for step in range(1, sub_count):
        block = projected.at[front, mine, :]
        remote(block, block, sub_send.at[step], sub_recv.at[sub], "sub", lax.rem(sub + step, sub_count)).wait_send()
    for step in range(1, front_count):
        block = projected.at[front]
        remote(
            block, block, front_send.at[step], front_recv.at[front], "front", lax.rem(front + step, front_count)
        ).wait_send()
    for peer in range(last):

        @pl.when(jnp.logical_and(peer < front, front < last))
        def _():
            block = mixings.at[front]
            remote(block, block, mixing_send.at[peer], mixing_recv.at[front], "front", peer).wait_send()

        @pl.when(peer < front)
        def _():
            block = openings.at[front]
            remote(block, block, opening_send.at[peer], opening_recv.at[front], "front", peer).wait_send()

    root_store.wait()
    for store in stores:
        store.wait()


def body(
    front_count,
    sub_count,
    noise_root,
    inverse_root,
    up_root,
    left_root,
    rank_root,
    basis_root,
    noise_child,
    inverse_child,
    up_child,
    left_child,
    rank_child,
    couple,
    pattern,
    couple_rank,
):
    share = noise_root.shape[1]
    child_tiles, samples, _ = noise_child.shape
    order, width = up_root.shape[1:]
    couplings = couple.shape[1]
    arrays = (
        noise_root,
        inverse_root,
        up_root,
        left_root,
        basis_root,
        noise_child,
        inverse_child,
        up_child,
        left_child,
        couple,
    )
    dma = pltpu.SemaphoreType.DMA
    return pl.pallas_call(
        functools.partial(kernel, front_count, sub_count),
        out_shape=(
            pltpu.VMEM(noise_root.shape, F32),
            pltpu.VMEM(noise_child.shape, F32),
        ),
        in_specs=[pl.BlockSpec(memory_space=pltpu.HBM)] * (4 + len(arrays)),
        out_specs=(pl.BlockSpec(memory_space=pl.ANY), pl.BlockSpec(memory_space=pl.ANY)),
        scratch_shapes=[pltpu.SMEM(array.shape, jnp.int32) for array in (rank_root, rank_child, pattern, couple_rank)]
        + [pltpu.VMEM(array.shape, F32) for array in arrays[:-1]]
        + [
            pltpu.VMEM(couple.shape[1:], F32),
            pltpu.VMEM(noise_root.shape, F32),
            pltpu.VMEM(noise_child.shape, F32),
            pltpu.VMEM((2 * width, width), F32),
            pltpu.VMEM((share, width), F32),
            pltpu.VMEM((share, width), F32),
            pltpu.VMEM((front_count, samples, width), F32),
            pltpu.VMEM((samples, width), F32),
            pltpu.VMEM((width, (1 + couplings) * width), F32),
            pltpu.VMEM((child_tiles, width, order), BF16),
            pltpu.VMEM((child_tiles, width, order), BF16),
            pltpu.VMEM((front_count, width, width), F32),
            pltpu.VMEM((front_count, samples, width), F32),
            pltpu.VMEM((samples, width), F32),
            dma((4 + len(arrays),)),
            dma((1 + child_tiles,)),
            dma((2,)),
            dma((sub_count,)),
            dma((sub_count,)),
            dma((front_count,)),
            dma((front_count,)),
            dma((front_count,)),
            dma((front_count,)),
            dma((front_count,)),
            dma((front_count,)),
        ],
        compiler_params=pltpu.CompilerParams(
            collective_id=0, has_side_effects=True, vmem_limit_bytes=64 * 1024 * 1024 - 4 * (noise_root.size + noise_child.size) - (1 << 20)
        ),
        name="matern_sample",
    )(rank_root, rank_child, pattern, couple_rank, *arrays)


def solution(mesh):
    placed = (
        P("front", "sub", None),
        P("front", None, None),
        P("front", None, None),
        P("front", None, None),
        P("front"),
        P("front", None, None),
        P(("sub", "front"), None, None),
        P(("sub", "front"), None, None),
        P(("sub", "front"), None, None),
        P(("sub", "front"), None, None),
        P(("sub", "front")),
        P(("sub", "front"), None, None, None, None),
        P(("sub", "front"), None),
        P(("sub", "front"), None),
    )
    return jax.shard_map(
        functools.partial(body, mesh.shape["front"], mesh.shape["sub"]),
        mesh=mesh,
        in_specs=placed,
        out_specs=(P("front", "sub", None), P(("sub", "front"), None, None)),
        check_vma=False,
    )
```

```python
import functools

import jax
import jax.numpy as jnp
from jax import lax
from jax.experimental import pallas as pl
from jax.experimental.pallas import tpu as pltpu
from jax.sharding import PartitionSpec as P

F32 = jnp.float32
BF16 = jnp.bfloat16
NN = ((1,), (0,))
NT = ((1,), (1,))


def split(value):
    high = value.astype(BF16)
    return high, (value - high.astype(F32)).astype(BF16)


def dot3(left, right, contract):
    def one(x, y):
        return lax.dot_general(x, y, (contract, ((), ())), preferred_element_type=F32)

    rows = left[0].shape[0]
    side = 1 - contract[1][0]
    columns = right[0].shape[side]
    stacked = jnp.concatenate(left, axis=0)
    if columns <= 128:
        both = one(stacked, jnp.concatenate(right, axis=side))
        return both[:rows, :columns] + (both[rows:, :columns] + both[:rows, columns:])
    both = one(stacked, right[0])
    return both[:rows] + (both[rows:] + one(left[0], right[1]))


def dot(left, right, contract):
    return dot3(split(left), split(right), contract)


def kernel(
    front_count,
    sub_count,
    rank_root_hbm,
    rank_child_hbm,
    pattern_hbm,
    couple_rank_hbm,
    noise_root_hbm,
    inverse_root_hbm,
    up_root_hbm,
    left_root_hbm,
    basis_root_hbm,
    noise_child_hbm,
    inverse_child_hbm,
    up_child_hbm,
    left_child_hbm,
    couple_hbm,
    solved_root_hbm,
    solved_child_hbm,
    rank_root,
    rank_child,
    pattern,
    couple_rank,
    noise_root,
    inverse_root,
    up_root,
    left_root,
    basis_root,
    noise_child,
    inverse_child,
    up_child,
    left_child,
    couple,
    solved_root,
    solved_child,
    root_message,
    root_outgoing,
    projected,
    child_opening,
    child_factor,
    carried_high,
    carried_low,
    mixings,
    openings,
    message,
    load_sem,
    store_sem,
    chain_sem,
    sub_send,
    sub_recv,
    front_send,
    front_recv,
    mixing_send,
    mixing_recv,
    opening_send,
    opening_recv,
):
    sub = lax.axis_index("sub")
    front = lax.axis_index("front")
    root_tiles, share, _ = noise_root.shape
    child_tiles = noise_child.shape[0]
    width = up_root.shape[-1]
    couplings = couple.shape[0]
    last = front_count - 1

    loads = {}
    for index, (name, source, target) in enumerate((
        ("rank_root", rank_root_hbm, rank_root),
        ("rank_child", rank_child_hbm, rank_child),
        ("pattern", pattern_hbm, pattern),
        ("couple_rank", couple_rank_hbm, couple_rank),
        ("inverse_root", inverse_root_hbm, inverse_root),
        ("up_root", up_root_hbm, up_root),
        ("basis_root", basis_root_hbm, basis_root),
        ("noise_root", noise_root_hbm, noise_root),
        ("left_root", left_root_hbm, left_root),
        ("inverse_child", inverse_child_hbm, inverse_child),
        ("up_child", up_child_hbm, up_child),
        ("noise_child", noise_child_hbm, noise_child),
        ("left_child", left_child_hbm, left_child),
        ("couple", couple_hbm.at[0], couple),
    )):
        loads[name] = pltpu.make_async_copy(source, target, load_sem.at[index])
        loads[name].start()

    barrier = pltpu.get_barrier_semaphore()
    for step in range(1, sub_count):
        pl.semaphore_signal(
            barrier, inc=1, device_id={"sub": lax.rem(sub + step, sub_count)}, device_id_type=pl.DeviceIdType.MESH
        )
    for step in range(1, front_count):
        pl.semaphore_signal(
            barrier, inc=1, device_id={"front": lax.rem(front + step, front_count)}, device_id_type=pl.DeviceIdType.MESH
        )

    lanes = lax.broadcasted_iota(jnp.int32, (1, width), 1)
    rows = lax.broadcasted_iota(jnp.int32, (width, width), 0)
    for name in ("rank_root", "rank_child", "pattern", "couple_rank"):
        loads[name].wait()
    root_keep = (lanes < rank_root[0]).astype(F32)
    child_keep = (lanes < rank_child[0]).astype(F32)

    def remote(source, target, send, recv, axis, peer):
        return pltpu.make_async_remote_copy(
            src_ref=source,
            dst_ref=target,
            send_sem=send,
            recv_sem=recv,
            device_id={axis: peer},
            device_id_type=pl.DeviceIdType.MESH,
        )

    for name in ("inverse_root", "up_root", "basis_root", "noise_root"):
        loads[name].wait()
    solved_bases = []
    opening = jnp.zeros((share, 2 * width), F32)
    for tile in range(root_tiles):
        bases = jnp.concatenate([up_root[tile], basis_root[tile]], axis=1)
        solved_basis = dot(inverse_root[tile], bases, NN)
        opening = opening + dot(noise_root[tile], solved_basis, NN)
        solved_bases.append(solved_basis)
    pl.semaphore_wait(barrier, sub_count + front_count - 2)

    chain = remote(
        root_outgoing, root_message, chain_sem.at[0], chain_sem.at[1], "front", lax.rem(front + last, front_count)
    )

    @pl.when(front == last)
    def _():
        root_message[...] = jnp.zeros_like(root_message)
        root_outgoing[...] = root_keep * opening[:, :width]
        chain.start()

    loads["left_root"].wait()
    mixing = jnp.zeros((2 * width, width), F32)
    for tile in range(root_tiles):
        mixing = mixing + dot(solved_bases[tile].T, left_root[tile], NN)
    mixing = split(mixing.T)

    @pl.when(front < last)
    def _():
        chain.wait_recv()

    arrived = root_message[...]
    both = opening - dot3(split(arrived), mixing, NN)

    @pl.when(jnp.logical_and(front < last, front > 0))
    def _():
        root_outgoing[...] = root_keep * both[:, :width]
        chain.start()

    mine = pl.ds(pl.multiple_of(sub * share, share), share)
    projected[front, mine, :] = both[:, width:]
    for step in range(1, sub_count):
        block = projected.at[front, mine, :]
        remote(block, block, sub_send.at[step], sub_recv.at[sub], "sub", lax.rem(sub + step, sub_count)).start()

    for name in ("inverse_child", "up_child", "noise_child", "left_child", "couple"):
        loads[name].wait()
    child_opening[...] = jnp.zeros_like(child_opening)
    child_factor[...] = jnp.zeros_like(child_factor)

    def prepare(tile, _):
        solved_basis = dot(inverse_child[tile], up_child[tile], NN)
        child_opening[...] += dot(noise_child[tile], solved_basis, NN)
        columns = jnp.concatenate([left_child[tile]] + [couple[m, tile] for m in range(couplings)], axis=1)
        child_factor[...] += dot(solved_basis.T, columns, NN)
        return 0

    def handed(step, pair, peer, panel):
        block = projected.at[panel, pl.ds(pl.multiple_of(pair * 2 * share, 2 * share), 2 * share), :]
        return remote(block, block, front_send.at[pair, step], front_recv.at[pair, panel], "front", peer)

    pairs = sub_count // 2
    for turn in range(pairs):
        pair = lax.rem(sub // 2 + turn, pairs)
        peers = [2 * pair, 2 * pair + 1] if turn > 0 else [sub + 1 - 2 * lax.rem(sub, 2)]
        for peer in peers:
            block = projected.at[front, pl.ds(pl.multiple_of(peer * share, share), share), :]
            remote(block, block, sub_send.at[0], sub_recv.at[peer], "sub", peer).wait_recv()
        for step in range(1, front_count):
            handed(step, pair, lax.rem(front + step, front_count), front).start()
        lax.fori_loop(child_tiles * turn // pairs, child_tiles * (turn + 1) // pairs, prepare, 0)

    mixings[front] = jnp.where(rows < rank_child[0], -child_factor[:, :width], 0.0)
    for peer in range(last):

        @pl.when(jnp.logical_and(peer < front, front < last))
        def _():
            block = mixings.at[front]
            remote(block, block, mixing_send.at[peer], mixing_recv.at[front], "front", peer).start()

    for tile in range(root_tiles):
        reduced = noise_root[tile] - dot(arrived, left_root[tile], NT)
        solved_root[tile] = dot(reduced, inverse_root[tile], NN)
    root_store = pltpu.make_async_copy(solved_root, solved_root_hbm, store_sem.at[0])
    root_store.start()

    factor = split(child_factor[:, width:])
    for step in range(1, front_count):
        peer = lax.rem(front + step, front_count)
        for pair in range(pairs):
            handed(step, pair, peer, peer).wait_recv()

    chosen = jnp.concatenate(
        [
            projected[pattern[0, m]] * (lanes < couple_rank[0, m]).astype(F32)
            for m in range(couplings)
        ],
        axis=1,
    )
    chosen = split(chosen)
    openings[front] = child_keep * (child_opening[...] - dot3(chosen, factor, NT))
    for peer in range(last):

        @pl.when(peer < front)
        def _():
            block = openings.at[front]
            remote(block, block, opening_send.at[peer], opening_recv.at[front], "front", peer).start()

    def solve(tile, _):
        inverse = split(inverse_child[tile])
        columns = jnp.concatenate([couple[m, tile] for m in range(couplings)], axis=1)
        source = noise_child[tile] - dot3(chosen, split(columns), NT)
        together = dot3(split(jnp.concatenate([source, left_child[tile].T], axis=0)), inverse, NN)
        solved_child[tile] = together[: source.shape[0]]
        carried_high[tile], carried_low[tile] = split(together[source.shape[0] :])
        return 0

    lax.fori_loop(0, child_tiles, solve, 0)

    message[...] = jnp.zeros_like(message)
    for panel in range(last, 0, -1):

        @pl.when(front < panel)
        def _():
            if panel < last:
                block = mixings.at[panel]
                remote(block, block, mixing_send.at[0], mixing_recv.at[panel], "front", panel).wait_recv()
            block = openings.at[panel]
            remote(block, block, opening_send.at[0], opening_recv.at[panel], "front", panel).wait_recv()
            if panel < last:
                message[...] = openings[panel] + dot(message[...], mixings[panel], NT)
            else:
                message[...] = openings[panel]

    incoming = split(message[...])
    stores = []
    for tile in range(child_tiles):
        solved_child[tile] -= dot3(incoming, (carried_high[tile], carried_low[tile]), NN)
        stores.append(pltpu.make_async_copy(solved_child.at[tile], solved_child_hbm.at[tile], store_sem.at[1 + tile]))
        stores[-1].start()

    @pl.when(front > 0)
    def _():
        chain.wait_send()

    for step in range(1, sub_count):
        block = projected.at[front, mine, :]
        remote(block, block, sub_send.at[step], sub_recv.at[sub], "sub", lax.rem(sub + step, sub_count)).wait_send()
    for step in range(1, front_count):
        for pair in range(pairs):
            handed(step, pair, lax.rem(front + step, front_count), front).wait_send()
    for peer in range(last):

        @pl.when(jnp.logical_and(peer < front, front < last))
        def _():
            block = mixings.at[front]
            remote(block, block, mixing_send.at[peer], mixing_recv.at[front], "front", peer).wait_send()

        @pl.when(peer < front)
        def _():
            block = openings.at[front]
            remote(block, block, opening_send.at[peer], opening_recv.at[front], "front", peer).wait_send()

    root_store.wait()
    for store in stores:
        store.wait()


def body(
    front_count,
    sub_count,
    noise_root,
    inverse_root,
    up_root,
    left_root,
    rank_root,
    basis_root,
    noise_child,
    inverse_child,
    up_child,
    left_child,
    rank_child,
    couple,
    pattern,
    couple_rank,
):
    share = noise_root.shape[1]
    child_tiles, samples, _ = noise_child.shape
    order, width = up_root.shape[1:]
    couplings = couple.shape[1]
    arrays = (
        noise_root,
        inverse_root,
        up_root,
        left_root,
        basis_root,
        noise_child,
        inverse_child,
        up_child,
        left_child,
        couple,
    )
    dma = pltpu.SemaphoreType.DMA
    return pl.pallas_call(
        functools.partial(kernel, front_count, sub_count),
        out_shape=(
            pltpu.VMEM(noise_root.shape, F32),
            pltpu.VMEM(noise_child.shape, F32),
        ),
        in_specs=[pl.BlockSpec(memory_space=pltpu.HBM)] * (4 + len(arrays)),
        out_specs=(pl.BlockSpec(memory_space=pl.ANY), pl.BlockSpec(memory_space=pl.ANY)),
        scratch_shapes=[pltpu.SMEM(array.shape, jnp.int32) for array in (rank_root, rank_child, pattern, couple_rank)]
        + [pltpu.VMEM(array.shape, F32) for array in arrays[:-1]]
        + [
            pltpu.VMEM(couple.shape[1:], F32),
            pltpu.VMEM(noise_root.shape, F32),
            pltpu.VMEM(noise_child.shape, F32),
            pltpu.VMEM((share, width), F32),
            pltpu.VMEM((share, width), F32),
            pltpu.VMEM((front_count, samples, width), F32),
            pltpu.VMEM((samples, width), F32),
            pltpu.VMEM((width, (1 + couplings) * width), F32),
            pltpu.VMEM((child_tiles, width, order), BF16),
            pltpu.VMEM((child_tiles, width, order), BF16),
            pltpu.VMEM((front_count, width, width), F32),
            pltpu.VMEM((front_count, samples, width), F32),
            pltpu.VMEM((samples, width), F32),
            dma((4 + len(arrays),)),
            dma((1 + child_tiles,)),
            dma((2,)),
            dma((sub_count,)),
            dma((sub_count,)),
            dma((sub_count // 2, front_count)),
            dma((sub_count // 2, front_count)),
            dma((front_count,)),
            dma((front_count,)),
            dma((front_count,)),
            dma((front_count,)),
        ],
        compiler_params=pltpu.CompilerParams(
            collective_id=0, has_side_effects=True, vmem_limit_bytes=64 * 1024 * 1024 - 4 * (noise_root.size + noise_child.size) - (1 << 20)
        ),
        name="matern_sample",
    )(rank_root, rank_child, pattern, couple_rank, *arrays)


def solution(mesh):
    placed = (
        P("front", "sub", None),
        P("front", None, None),
        P("front", None, None),
        P("front", None, None),
        P("front"),
        P("front", None, None),
        P(("sub", "front"), None, None),
        P(("sub", "front"), None, None),
        P(("sub", "front"), None, None),
        P(("sub", "front"), None, None),
        P(("sub", "front")),
        P(("sub", "front"), None, None, None, None),
        P(("sub", "front"), None),
        P(("sub", "front"), None),
    )
    return jax.shard_map(
        functools.partial(body, mesh.shape["front"], mesh.shape["sub"]),
        mesh=mesh,
        in_specs=placed,
        out_specs=(P("front", "sub", None), P(("sub", "front"), None, None)),
        check_vma=False,
    )
```
